32 devices in a mesh: node: 8 (over y, x, core), local: 4 (over z).
Axes of the slice: x: 2, y: 2, z: 4, core: 2. Of those that a mesh axis runs over, the one named last changes fastest.
Arguments:
- tokens: bfloat16 [4096, 2048], P(('node', 'local')), may hold values from -6 to 6
- route: int32 [4096, 4], P(('node', 'local')), may hold values from 0 to 63, all different within a row; in each aligned block of 128 rows (0 to 127, 128 to 255, ...) at most 9 rows name the same one
- combine_weights: float32 [4096, 4], P(('node', 'local')), may hold values from 0.05 to 1
- w_gate: bfloat16 [64, 2048, 1408], P('node', None, 'local'), may hold values from -0.125 to 0.125
- w_up: bfloat16 [64, 2048, 1408], P('node', None, 'local'), may hold values from -0.125 to 0.125
- w_down: bfloat16 [64, 1408, 2048], P('node', 'local'), may hold values from -0.15625 to 0.15625
- grad_out: bfloat16 [4096, 2048], P(('node', 'local')), may hold values from -6 to 6
Outputs:
- combined: bfloat16 [4096, 2048], P(('node', 'local'))
- d_tokens: bfloat16 [4096, 2048], P(('node', 'local'))
- d_weights: float32 [4096, 4], P(('node', 'local'))
The draws below stay inside these ranges and needn't reach their ends.
Inputs may be any that keep to these rules, and one draw needn't show every extreme that they name: `route`: the 4 experts of one token differ; within the 128 tokens of one device no expert is named more than 9 times, and some device names some expert exactly 9 times.
All inputs are finite; a program needn't handle non-finite values.
Results may differ from the reference program's by a relative error of at most 0.012.
Values may be sent and summed in bfloat16 or wider, within the bound.
A program may use at most 192 MiB of HBM per device.

```python
import math
import jax
import jax.numpy as jnp
import numpy as np
from jax import lax

D = 2048
FF = 1408
EXPERTS = 64
TOP = 4
TOK_DEV = 128
CAP = 9
TOKENS = 4096
HID = 352


def levels(stream_key, extent, shards, least, high):
    level, own = 1.0, jax.random.fold_in(stream_key, 6)
    for axis_at, blocks in shards:
        draws = jnp.exp(jax.random.uniform(jax.random.fold_in(own, axis_at), (blocks,), jnp.float32, least / len(shards), high / len(shards)))
        level = level * jnp.repeat(draws, extent[axis_at] // blocks).reshape([-1 if axis == axis_at else 1 for axis in range(len(extent))])
    return level


def shared_out(key, own, number, rows, count, top, most, lean):
    sequence = jax.random.permutation(key, count)
    packed, usual = shares(count, rows * top, most, lean, True), shares(count, rows * top, most, lean, False)
    places = jnp.arange(count)

    def named(lengths, rotation):
        used = int((lengths > 0).sum())
        fixed = max(1, used // 4)
        shifted = fixed + (places - fixed + rotation * (used - fixed)) % max(1, count - fixed)
        return jnp.zeros((count,), jnp.int32).at[sequence[jnp.where(places < fixed, places, shifted)]].set(jnp.asarray(lengths, jnp.int32))

    lengths = jnp.where(number % 4 == 0, named(packed, number // 4), named(usual, number - number // 4 - 1))
    mixed = jax.random.permutation(jax.random.fold_in(own, 3), count)
    source_of, taker = mixed[0:count // 2 * 2:2], mixed[1:count // 2 * 2:2]
    room = jnp.minimum(lengths[source_of] - 1, most - lengths[taker]) // 2
    room = jnp.where((source_of == sequence[0]) | (taker == sequence[0]) | (lengths[taker] == 0), 0, jnp.maximum(room, 0))
    shifted = jax.random.randint(jax.random.fold_in(own, 4), (count // 2,), 0, 1 << 20) % (room + 1)
    lengths = lengths.at[source_of].add(-shifted).at[taker].add(shifted)
    members = jnp.searchsorted(jnp.cumsum(lengths), jnp.arange(rows * top), side="right").astype(jnp.int32)
    table = members.reshape(top, rows).T
    table = table[jax.random.permutation(jax.random.fold_in(own, 1), rows)]
    rotation = jax.random.randint(jax.random.fold_in(own, 2), (rows, 1), 0, top)
    return jnp.take_along_axis(table, (jnp.arange(top)[None, :] + rotation) % top, axis=1)


def shares(count, total, most, lean, full):
    weights = [(1 << 20) // math.isqrt(rank ** lean) + 1 for rank in range(1, count + 1)]
    largest = most if full else min(most, max(-(-total // count), total * weights[0] // sum(weights)))
    least = 1 if total - largest >= count - 1 else 0
    holding, spare = [largest] + [least] * (count - 1), total - largest - least * (count - 1)
    while spare > 0:
        candidates = [i for i in range(1, count) if holding[i] < largest] or [i for i in range(1, count) if holding[i] < most]
        pool, budget = sum([weights[i] for i in candidates]), spare
        for i in candidates:
            extra = min(most - holding[i], max(1, budget * weights[i] // pool), spare)
            holding[i] = holding[i] + extra
            spare = spare - extra
    return np.array(holding)


def scatter_about(rng, shape, scale, limit, split=(), kind=jnp.bfloat16):
    loudness = levels(rng, shape, split, -0.22, 0.18) if split else 1.0
    array = jax.random.normal(rng, shape, jnp.float32) * scale * loudness
    return jnp.minimum(jnp.maximum(array, -limit), limit).astype(kind)


def setup_inputs(seed: int = 0) -> dict:
    keys = jax.random.split(jax.random.key(seed), 8)
    tokens = scatter_about(keys[0], (TOKENS, D), 1.0, 6.0, ((0, 32),))
    route_keys = jax.random.split(jax.random.fold_in(keys[1], 1), TOKENS // TOK_DEV)
    route_turns = jax.random.permutation(jax.random.fold_in(keys[1], 3), TOKENS // TOK_DEV)
    route = jax.vmap(lambda own, number: shared_out(jax.random.fold_in(keys[1], 2), own, number, TOK_DEV, EXPERTS, TOP, CAP, 2))(route_keys, route_turns).reshape((TOKENS, TOP))
    combine_weights = jnp.clip(0.05 + 0.95 * jax.random.uniform(keys[2], (TOKENS, TOP), jnp.float32) ** levels(keys[2], (TOKENS, TOP), ((0, 32),), -0.2, 0.2), 0.05, 1.0)
    w_gate = scatter_about(keys[3], (EXPERTS, D, FF), D ** -0.5, 0.125, ((0, 8), (2, 4)))
    w_up = scatter_about(keys[4], (EXPERTS, D, FF), D ** -0.5, 0.125, ((0, 8), (2, 4)))
    w_down = scatter_about(keys[5], (EXPERTS, FF, D), FF ** -0.5, 0.15625, ((0, 8), (1, 4)))
    grad_out = scatter_about(keys[6], (TOKENS, D), 1.0, 6.0, ((0, 32),))
    return dict(tokens=tokens, route=route, combine_weights=combine_weights, w_gate=w_gate, w_up=w_up, w_down=w_down, grad_out=grad_out)


def place_pairs(route_block):
    flat_routes = route_block.reshape(-1)
    one_hot = (flat_routes[:, None] == jnp.arange(EXPERTS, dtype=jnp.int32)[None, :]).astype(jnp.int32)
    earlier = jnp.cumsum(one_hot, axis=0) - one_hot
    slot_rank = jnp.sum(earlier * one_hot, axis=1)
    return (flat_routes * CAP + slot_rank).astype(jnp.int32)


def round_trip(value):
    return lax.optimization_barrier(value.astype(jnp.bfloat16)).astype(jnp.float32)


def one_expert(expert_args):
    token_rows, grad_rows, gate_weight, up_weight, down_weight = expert_args
    gate_val = jnp.dot(token_rows, gate_weight, preferred_element_type=jnp.float32)
    up_val = jnp.dot(token_rows, up_weight, preferred_element_type=jnp.float32)
    hidden = (jax.nn.silu(gate_val) * up_val).astype(jnp.bfloat16)
    d_hidden = jnp.dot(grad_rows, down_weight.T, preferred_element_type=jnp.float32)
    sigmoid_gate = jax.nn.sigmoid(gate_val)
    d_gate = (d_hidden * up_val * sigmoid_gate * (1.0 + gate_val * (1.0 - sigmoid_gate))).astype(jnp.bfloat16)
    d_up = (d_hidden * gate_val * sigmoid_gate).astype(jnp.bfloat16)
    out_total = jnp.zeros((token_rows.shape[0], D), jnp.float32)
    back_total = jnp.zeros((token_rows.shape[0], D), jnp.float32)
    for block_index in range(FF // HID):
        lower_edge = block_index * HID
        upper_edge = lower_edge + HID
        out_total = out_total + round_trip(jnp.dot(hidden[:, lower_edge:upper_edge], down_weight[lower_edge:upper_edge], preferred_element_type=jnp.float32))
        back_term = jnp.dot(d_gate[:, lower_edge:upper_edge], gate_weight[:, lower_edge:upper_edge].T, preferred_element_type=jnp.float32) + jnp.dot(d_up[:, lower_edge:upper_edge], up_weight[:, lower_edge:upper_edge].T, preferred_element_type=jnp.float32)
        back_total = back_total + round_trip(back_term)
    return out_total.astype(jnp.bfloat16), back_total.astype(jnp.bfloat16)


def reference(tokens, route, combine_weights, w_gate, w_up, w_down, grad_out):
    devices = TOKENS // TOK_DEV
    pair_count = TOK_DEV * TOP
    tok_blocks = tokens.reshape(devices, TOK_DEV, D)
    position = jax.vmap(place_pairs)(route.reshape(devices, pair_count))
    dev_index = jnp.arange(devices, dtype=jnp.int32)[:, None]
    pair_tokens = jnp.repeat(tok_blocks, TOP, axis=1)
    buffer_x = jnp.zeros((devices, EXPERTS * CAP, D), jnp.bfloat16).at[dev_index, position].set(pair_tokens)
    weight_blocks = combine_weights.reshape(devices, TOK_DEV, TOP)
    grad_blocks = grad_out.reshape(devices, TOK_DEV, D)
    grad_pairs = (weight_blocks[:, :, :, None] * grad_blocks[:, :, None, :].astype(jnp.float32)).astype(jnp.bfloat16).reshape(devices, pair_count, D)
    buffer_g = jnp.zeros((devices, EXPERTS * CAP, D), jnp.bfloat16).at[dev_index, position].set(grad_pairs)
    by_expert_x = buffer_x.reshape(devices, EXPERTS, CAP, D).transpose(1, 0, 2, 3).reshape(EXPERTS, devices * CAP, D)
    by_expert_g = buffer_g.reshape(devices, EXPERTS, CAP, D).transpose(1, 0, 2, 3).reshape(EXPERTS, devices * CAP, D)
    expert_out, expert_back = lax.map(one_expert, (by_expert_x, by_expert_g, w_gate, w_up, w_down))
    out_rows = expert_out.reshape(EXPERTS, devices, CAP, D).transpose(1, 0, 2, 3).reshape(devices, EXPERTS * CAP, D)
    back_rows = expert_back.reshape(EXPERTS, devices, CAP, D).transpose(1, 0, 2, 3).reshape(devices, EXPERTS * CAP, D)
    pair_out = jnp.take_along_axis(out_rows, position[:, :, None], axis=1).reshape(devices, TOK_DEV, TOP, D).astype(jnp.float32)
    pair_back = jnp.take_along_axis(back_rows, position[:, :, None], axis=1).reshape(devices, TOK_DEV, TOP, D).astype(jnp.float32)
    combined = jnp.sum(weight_blocks[:, :, :, None] * pair_out, axis=2).astype(jnp.bfloat16).reshape(TOKENS, D)
    d_weights = jnp.einsum("ntkd,ntd->ntk", pair_out, grad_blocks.astype(jnp.float32), precision=lax.Precision.HIGHEST).reshape(TOKENS, TOP)
    d_tokens = jnp.sum(pair_back, axis=2).astype(jnp.bfloat16).reshape(TOKENS, D)
    return combined, d_tokens, d_weights
```

```python
import functools

import jax
import jax.numpy as jnp
from jax import lax
from jax.experimental import pallas as pl
from jax.experimental.pallas import tpu as pltpu
from jax.sharding import PartitionSpec as P

EXPERTS = 64
TOP = 4
CAP = 9


def place_pairs(route):
    flat_routes = route.reshape(-1)
    one_hot = (flat_routes[:, None] == jnp.arange(EXPERTS, dtype=jnp.int32)[None, :]).astype(
        jnp.int32
    )
    earlier = jnp.cumsum(one_hot, axis=0) - one_hot
    slot_rank = jnp.sum(earlier * one_hot, axis=1)
    return flat_routes * CAP + slot_rank


def routed_plan(tokens, route, combine_weights, w_gate, w_up, w_down, grad_out):
    node_count = lax.axis_size("node")
    tok_rows, model_width = tokens.shape
    per_node = w_gate.shape[0]
    pair_rows = tok_rows * TOP
    position = place_pairs(route)
    targets = (jnp.arange(EXPERTS * CAP, dtype=jnp.int32)[:, None] == position[None, :]).astype(
        jnp.bfloat16
    )
    token_targets = targets.reshape(EXPERTS * CAP, tok_rows, TOP).sum(axis=2)
    full_gate, full_up, full_down = (w_gate, w_up, w_down)
    hidden_width = full_gate.shape[2]
    w_inner = jnp.concatenate([full_gate, full_up], axis=2)

    def dispatch(send_rows, worker):
        outgoing = send_rows.reshape(node_count, per_node, CAP, model_width)
        arrived = lax.all_to_all(outgoing, "node", split_axis=0, concat_axis=0, tiled=True)
        return worker(lax.all_gather(arrived[None], "local", axis=0, tiled=True), jnp.int32(0))

    def combine(term_fn):
        summed = lax.psum_scatter(
            term_fn(jnp.int32(0), 1 * lax.axis_size("local")).astype(jnp.bfloat16),
            "local",
            scatter_dimension=0,
            tiled=True,
        ).astype(jnp.float32)
        returned = lax.all_to_all(
            summed[0].astype(jnp.bfloat16), "node", split_axis=0, concat_axis=0, tiled=True
        )
        return returned.reshape(EXPERTS * CAP, model_width)

    send_tokens = jnp.dot(token_targets, tokens, preferred_element_type=jnp.float32).astype(
        jnp.bfloat16
    )

    def forward_work(block_rows, first_row):
        return jnp.einsum(
            "abecd,edh->abech", block_rows, w_inner, preferred_element_type=jnp.float32
        )

    gate_up = dispatch(send_tokens, forward_work)
    hidden = (jax.nn.silu(gate_up[..., :hidden_width]) * gate_up[..., hidden_width:]).astype(
        jnp.bfloat16
    )

    def down_term(first_row, row_count):
        return jnp.einsum("abech,ehd->abecd", hidden, full_down, preferred_element_type=jnp.float32)

    expert_out = combine(down_term)
    pair_view = expert_out[position].reshape(tok_rows, TOP, model_width)
    combined = jnp.sum(combine_weights[:, :, None] * pair_view.astype(jnp.float32), axis=1).astype(
        jnp.bfloat16
    )
    d_weights = jnp.einsum("tkd,td->tk", pair_view, grad_out, preferred_element_type=jnp.float32)
    grad_pairs = (
        (combine_weights[:, :, None] * grad_out[:, None, :].astype(jnp.float32))
        .astype(jnp.bfloat16)
        .reshape(pair_rows, model_width)
    )
    send_grads = jnp.dot(targets, grad_pairs, preferred_element_type=jnp.float32).astype(
        jnp.bfloat16
    )

    def backward_work(block_rows, first_row):
        d_hidden = jnp.einsum(
            "abecd,ehd->abech", block_rows, full_down, preferred_element_type=jnp.float32
        )
        gate_val = gate_up[..., :hidden_width]
        up_val = gate_up[..., hidden_width:]
        sigmoid_gate = jax.nn.sigmoid(gate_val)
        d_gate = d_hidden * up_val * sigmoid_gate * (1.0 + gate_val * (1.0 - sigmoid_gate))
        d_up = d_hidden * gate_val * sigmoid_gate
        return jnp.concatenate([d_gate.astype(jnp.bfloat16), d_up.astype(jnp.bfloat16)], axis=-1)

    d_inner = dispatch(send_grads, backward_work)

    def back_term(first_row, row_count):
        return jnp.einsum("abech,edh->abecd", d_inner, w_inner, preferred_element_type=jnp.float32)

    d_rows = combine(back_term)
    d_pairs = d_rows[position].reshape(tok_rows, TOP, model_width)
    d_tokens = jnp.sum(d_pairs.astype(jnp.float32), axis=1).astype(jnp.bfloat16)
    return (combined, d_tokens, d_weights)

MESH = pl.DeviceIdType.MESH
VMEM_LIMIT = 58 * 1024 * 1024
F32 = jnp.float32
BF16 = jnp.bfloat16


def place(nodes):
    n, z = lax.axis_index("node"), lax.axis_index("local")
    y, x, c = n // (nodes // 2), (n // (nodes // 4)) % 2, n % 2
    step_x = (nodes // 4) * (1 - 2 * x)
    step_y = (nodes // 2) * (1 - 2 * y)
    first = step_x * (1 - c) + step_y * c
    second = step_x * c + step_y * (1 - c)
    return n, z, 1 - 2 * c, first, second


def greet(n, z, locals_, steps):
    barrier = pltpu.get_barrier_semaphore()
    for step in steps:
        pl.semaphore_signal(barrier, inc=1, device_id=(n + step, z), device_id_type=MESH)
    for i in range(1, locals_):
        pl.semaphore_signal(
            barrier, inc=1, device_id=(n, (z + i) % locals_), device_id_type=MESH
        )
    pl.semaphore_wait(barrier, len(steps) + locals_ - 1)


def match_rows(meta, k, base, rows):
    ids = lax.broadcasted_iota(jnp.int32, (rows, meta.shape[1]), 0).astype(F32) + base
    return ids == meta[k : k + 1, :]


def gather_kernel(
    nodes, locals_, meta_ref, tok_ref, grad_ref, x_ref, g_ref, metas_ref, wr_ref,
    held, metas, pick, stage, own_sem, send_sem, recv_sem, stage_sem,
):
    n, z, sib, first, second = place(nodes)
    rows = x_ref.shape[1]
    base = (n * rows).astype(F32)
    loads = []
    me = n * locals_ + z
    for t, src in ((0, meta_ref), (1, tok_ref), (2, grad_ref)):
        dst = metas.at[me] if t == 0 else held.at[t - 1, me]
        copy = pltpu.make_async_copy(src, dst, own_sem.at[t])
        copy.start()
        loads.append(copy)
    greet(n, z, locals_, (sib, first, second))

    def block(t, index):
        return metas.at[index] if t == 0 else held.at[t - 1, index]

    def copy_of(t, index, slot, node, local):
        return pltpu.make_async_remote_copy(
            src_ref=block(t, index),
            dst_ref=block(t, index),
            send_sem=send_sem.at[t, slot],
            recv_sem=recv_sem.at[t, index],
            device_id=(node, local),
            device_id_type=MESH,
        )

    def arrived(t, index):
        copy_of(t, index, 0, n + sib, z).wait_recv()

    def at(step, i):
        return (n + step) * locals_ + (z + locals_ - i) % locals_

    slots = iter(range(3 * 64))
    counts = [0, 0, 0]

    def send(t, index, node, local):
        copy_of(t, index, counts[t], node, local).start()
        counts[t] += 1

    def phase_own(t):
        loads[t].wait()
        for i in range(1, locals_):
            send(t, me, n, (z + i) % locals_)
        send(t, me, n + second, z)
        send(t, me, n + first, z)
        send(t, me, n + sib, z)

    def phase_local(t):
        for i in range(1, locals_):
            index = at(0, i)
            arrived(t, index)
            send(t, index, n + second, z)
            send(t, index, n + first, z)
            send(t, index, n + sib, z)

    def phase_first(t):
        for i in range(locals_):
            index = at(first, i)
            arrived(t, index)
            send(t, index, n + second, z)
            send(t, index, n + sib, z)

    def phase_second(t, step):
        for i in range(locals_):
            index = at(step, i)
            arrived(t, index)
            send(t, index, n + sib, z)

    def from_sibling(t, step):
        for i in range(locals_):
            arrived(t, at(step, i))

    def dispatch(t, step, out_ref, order):
        group = n + step
        width = held.shape[2]
        for l in range(locals_):
            meta = metas[group * locals_ + l]
            hit = match_rows(meta, 0, base, rows)
            weight = jnp.where(hit, meta[TOP : TOP + 1, :], 0.0)
            for k in range(1, TOP):
                hit_k = match_rows(meta, k, base, rows)
                weight = jnp.where(hit_k, meta[TOP + k : TOP + k + 1, :], weight)
                hit = hit | hit_k
            pick[:, l * width : (l + 1) * width] = jnp.where(hit, 1.0, 0.0).astype(BF16)
            if t == 2:
                total = jnp.sum(weight, axis=1, keepdims=True)
                total = jnp.broadcast_to(total, (rows, wr_ref.shape[2]))
                if l == 0:
                    wr_ref[group] = total
                else:
                    wr_ref[group] = wr_ref[group] + total
        slot = order % 2
        out = pltpu.make_async_copy(stage.at[slot], out_ref.at[group], stage_sem.at[slot])
        if order >= 2:
            out.wait()
        tile = 512

        def columns(j, carry):
            cols = pl.ds(pl.multiple_of(j * tile, tile), tile)
            data = held[t - 1, pl.ds(group * locals_, locals_), :, cols]
            data = data.reshape(locals_ * width, tile)
            stage[slot, :, cols] = jnp.dot(
                pick[...], data, preferred_element_type=F32
            ).astype(BF16)
            return carry

        lax.fori_loop(0, held.shape[3] // tile, columns, 0)
        out.start()

    steps = (0, first, second, first + second)
    other = (sib, sib + second, sib + first, sib + first + second)
    phase_own(0)
    phase_own(1)
    phase_own(2)
    phase_local(0)
    phase_first(0)
    phase_local(1)
    phase_second(0, second)
    phase_second(0, first + second)
    for step in other:
        from_sibling(0, step)
    phase_first(1)
    phase_local(2)
    dispatch(1, 0, x_ref, 0)
    phase_second(1, second)
    phase_first(2)
    phase_second(1, first + second)
    from_sibling(1, other[0])
    dispatch(1, first, x_ref, 1)
    dispatch(1, second, x_ref, 2)
    dispatch(1, other[0], x_ref, 3)
    for j in range(1, 4):
        from_sibling(1, other[j])
    dispatch(1, first + second, x_ref, 4)
    dispatch(1, other[1], x_ref, 5)
    phase_second(2, second)
    dispatch(1, other[2], x_ref, 6)
    dispatch(1, other[3], x_ref, 7)
    dispatch(2, 0, g_ref, 8)
    dispatch(2, first, g_ref, 9)
    dispatch(2, second, g_ref, 10)
    from_sibling(2, other[0])
    dispatch(2, other[0], g_ref, 11)
    phase_second(2, first + second)
    from_sibling(2, other[1])
    from_sibling(2, other[2])
    dispatch(2, other[1], g_ref, 12)
    dispatch(2, other[2], g_ref, 13)
    dispatch(2, first + second, g_ref, 14)
    from_sibling(2, other[3])
    dispatch(2, other[3], g_ref, 15)
    metas_ref[...] = metas[...]
    for slot, order in ((0, 14), (1, 15)):
        pltpu.make_async_copy(stage.at[slot], g_ref.at[n], stage_sem.at[slot]).wait()
    for t in range(3):
        for s in range(counts[t]):
            copy_of(t, me, s, n + sib, z).wait_send()


def expert_kernel(x_ref, g_ref, wr_ref, wg_ref, wu_ref, wd_ref, y_ref, b_ref, dw_ref):
    groups, cap, width = x_ref.shape
    rows = groups * cap
    contract_last = (((1,), (1,)), ((), ()))
    x = x_ref[...].reshape(rows, width)
    g = g_ref[...].reshape(rows, width)
    w = wr_ref[...].reshape(rows, wr_ref.shape[2])[:, 0:1]
    gate = jnp.dot(x, wg_ref[0], preferred_element_type=F32)
    up = jnp.dot(x, wu_ref[0], preferred_element_type=F32)
    pull = lax.dot_general(g, wd_ref[0], contract_last, preferred_element_type=F32)
    s = 1.0 / (1.0 + jnp.exp(-gate))
    hidden = gate * s * up
    dw = jnp.sum(hidden.astype(BF16).astype(F32) * pull, axis=1, keepdims=True)
    dw_ref[...] = jnp.broadcast_to(dw, (rows, dw_ref.shape[2])).reshape(dw_ref.shape)
    pull = pull * w
    d_gate = (pull * up * s * (1.0 + gate * (1.0 - s))).astype(BF16)
    d_up = (pull * gate * s).astype(BF16)
    y = jnp.dot((hidden * w).astype(BF16), wd_ref[0], preferred_element_type=F32)
    y_ref[...] = y.astype(BF16).reshape(y_ref.shape)
    back = lax.dot_general(d_gate, wg_ref[0], contract_last, preferred_element_type=F32)
    back += lax.dot_general(d_up, wu_ref[0], contract_last, preferred_element_type=F32)
    b_ref[...] = back.astype(BF16).reshape(b_ref.shape)


def reduce_kernel(
    nodes, locals_, metas_ref, y_ref, out_ref,
    rows_in, pick, sib_send, sib_recv, hop_send, hop_recv, end_send, end_recv,
    load_sem, sib_sems, hop_sems, end_sems,
):
    n, z, sib, first, second = place(nodes)
    rows, model_width = y_ref.shape[1], y_ref.shape[2]
    width = out_ref.shape[0]
    base = (n * rows).astype(F32)
    order = (
        sib + first + second, sib + first, sib + second, sib,
        first + second, second, first, 0,
    )

    def load(j):
        return pltpu.make_async_copy(
            y_ref.at[n + order[j]], rows_in.at[j % 2], load_sem.at[j % 2]
        )

    load(0).start()
    greet(n, z, locals_, (sib, first, second))
    tile = 512
    tiles = model_width // tile

    def copy_to(src, dst, sems, s, node, local):
        return pltpu.make_async_remote_copy(
            src_ref=src,
            dst_ref=dst,
            send_sem=sems.at[0, s],
            recv_sem=sems.at[1, s],
            device_id=(node, local),
            device_id_type=MESH,
        )

    def sib_copy(j, l):
        s = j * locals_ + l
        return copy_to(sib_send.at[s], sib_recv.at[s], sib_sems, s, n + sib, z)

    def hop_copy(j, l):
        s = j * locals_ + l
        step = second if j < 2 else first
        return copy_to(hop_send.at[s], hop_recv.at[s], hop_sems, s, n + step, z)

    def end_copy(i):
        return copy_to(
            end_send.at[i], end_recv.at[i], end_sems, i, n, (z + i) % locals_
        )

    def part(j, l, addends, dst):
        meta = metas_ref[(n + order[j]) * locals_ + l]
        hit = match_rows(meta, 0, base, rows)
        for k in range(1, TOP):
            hit = hit | match_rows(meta, k, base, rows)
        pick[...] = jnp.where(hit, 1.0, 0.0).astype(BF16)

        def columns(q, carry):
            cols = pl.ds(pl.multiple_of(q * tile, tile), tile)
            total = lax.dot_general(
                pick[...], rows_in[j % 2, :, cols], (((0,), (0,)), ((), ())),
                preferred_element_type=F32,
            )
            for ref in addends:
                total = total + ref[:, cols].astype(F32)
            dst[:, cols] = total.astype(BF16)
            return carry

        lax.fori_loop(0, tiles, columns, 0)

    for j in range(8):
        load(j).wait()
        if j + 1 < 8:
            load(j + 1).start()
        for i in range(locals_):
            l = (z + i) % locals_
            m = i
            if j < 4:
                part(j, l, [], sib_send.at[j * locals_ + m])
                sib_copy(j, m).start()
                continue
            s = (j - 4) * locals_ + m
            sib_copy(j - 4, m).wait_recv()
            addends = [sib_recv.at[s]]
            if j == 6:
                hop_copy(0, m).wait_recv()
                addends.append(hop_recv.at[m])
            if j == 7:
                hop_copy(1, m).wait_recv()
                hop_copy(2, m).wait_recv()
                addends.append(hop_recv.at[locals_ + m])
                addends.append(hop_recv.at[2 * locals_ + m])
            if j < 7:
                part(j, l, addends, hop_send.at[s])
                hop_copy(j - 4, m).start()
            else:
                part(j, l, addends, end_send.at[m])
                if i > 0:
                    end_copy(i).start()
    for i in range(1, locals_):
        end_copy(i).wait_recv()

    def finish(q, carry):
        cols = pl.ds(pl.multiple_of(q * tile, tile), tile)
        total = end_send[0, :, cols].astype(F32)
        for i in range(1, locals_):
            total = total + end_recv[i, :, cols].astype(F32)
        out_ref[:, cols] = total.astype(BF16)
        return carry

    lax.fori_loop(0, tiles, finish, 0)
    for j in range(4):
        for m in range(locals_):
            sib_copy(j, m).wait_send()
    for j in range(3):
        for m in range(locals_):
            hop_copy(j, m).wait_send()
    for i in range(1, locals_):
        end_copy(i).wait_send()


def gathered_plan(tokens, route, combine_weights, w_gate, w_up, w_down, grad_out):
    nodes, locals_ = lax.axis_size("node"), lax.axis_size("local")
    tok_rows, model_width = tokens.shape
    per_node, _, hidden_width = w_gate.shape
    devices = nodes * locals_
    cap = -(-(locals_ * CAP) // 16) * 16
    rows = per_node * cap
    place_at = place_pairs(route)
    flat = route.reshape(-1)
    slot = place_at - flat * CAP
    row_id = flat * cap + lax.axis_index("local") * CAP + slot
    meta = jnp.concatenate(
        [row_id.reshape(tok_rows, TOP).T.astype(F32), combine_weights.T], axis=0
    )
    any_space = pl.BlockSpec(memory_space=pl.ANY)
    vmem_space = pl.BlockSpec(memory_space=pltpu.VMEM)
    x_rows, g_rows, metas, row_weights = pl.pallas_call(
        functools.partial(gather_kernel, nodes, locals_),
        out_shape=(
            jax.ShapeDtypeStruct((nodes, rows, model_width), BF16),
            jax.ShapeDtypeStruct((nodes, rows, model_width), BF16),
            jax.ShapeDtypeStruct((devices, 2 * TOP, tok_rows), F32),
            jax.ShapeDtypeStruct((nodes, rows, 128), F32),
        ),
        in_specs=[any_space] * 3,
        out_specs=(any_space, any_space, vmem_space, vmem_space),
        scratch_shapes=[
            pltpu.VMEM((2, devices, tok_rows, model_width), BF16),
            pltpu.VMEM((devices, 2 * TOP, tok_rows), F32),
            pltpu.VMEM((rows, locals_ * tok_rows), BF16),
            pltpu.VMEM((2, rows, model_width), BF16),
            pltpu.SemaphoreType.DMA((3,)),
            pltpu.SemaphoreType.DMA((3, devices)),
            pltpu.SemaphoreType.DMA((3, devices)),
            pltpu.SemaphoreType.DMA((2,)),
        ],
        compiler_params=pltpu.CompilerParams(
            collective_id=0, has_side_effects=True, vmem_limit_bytes=VMEM_LIMIT
        ),
    )(meta, tokens, grad_out)

    row_block = pl.BlockSpec((nodes, cap, model_width), lambda e: (0, e, 0))
    scalar_block = pl.BlockSpec((nodes, cap, 128), lambda e: (0, e, 0))
    tall = pl.BlockSpec((1, model_width, hidden_width), lambda e: (e, 0, 0))
    wide = pl.BlockSpec((1, hidden_width, model_width), lambda e: (e, 0, 0))
    y_rows, b_rows, d_row_weights = pl.pallas_call(
        expert_kernel,
        grid=(per_node,),
        out_shape=(
            jax.ShapeDtypeStruct((nodes, rows, model_width), BF16),
            jax.ShapeDtypeStruct((nodes, rows, model_width), BF16),
            jax.ShapeDtypeStruct((nodes, rows, 128), F32),
        ),
        in_specs=[row_block, row_block, scalar_block, tall, tall, wide],
        out_specs=(row_block, row_block, scalar_block),
        compiler_params=pltpu.CompilerParams(vmem_limit_bytes=VMEM_LIMIT),
    )(x_rows, g_rows, row_weights, w_gate, w_up, w_down)

    reduce_call = pl.pallas_call(
        functools.partial(reduce_kernel, nodes, locals_),
        out_shape=jax.ShapeDtypeStruct((tok_rows, model_width), BF16),
        in_specs=[vmem_space, any_space],
        out_specs=vmem_space,
        scratch_shapes=[
            pltpu.VMEM((2, rows, model_width), BF16),
            pltpu.VMEM((rows, tok_rows), BF16),
            pltpu.VMEM((4 * locals_, tok_rows, model_width), BF16),
            pltpu.VMEM((4 * locals_, tok_rows, model_width), BF16),
            pltpu.VMEM((3 * locals_, tok_rows, model_width), BF16),
            pltpu.VMEM((3 * locals_, tok_rows, model_width), BF16),
            pltpu.VMEM((locals_, tok_rows, model_width), BF16),
            pltpu.VMEM((locals_, tok_rows, model_width), BF16),
            pltpu.SemaphoreType.DMA((2,)),
            pltpu.SemaphoreType.DMA((2, 4 * locals_)),
            pltpu.SemaphoreType.DMA((2, 3 * locals_)),
            pltpu.SemaphoreType.DMA((2, locals_)),
        ],
        compiler_params=pltpu.CompilerParams(
            collective_id=1, has_side_effects=True, vmem_limit_bytes=VMEM_LIMIT
        ),
    )
    ids = metas[:, :TOP, :].reshape(nodes, locals_ * TOP * tok_rows)
    local_row = ids.astype(jnp.int32) - lax.axis_index("node") * rows
    named = local_row[:, :, None] == jnp.arange(rows, dtype=jnp.int32)[None, None, :]
    parts = jnp.sum(jnp.where(named, d_row_weights[:, None, :, 0], 0.0), axis=2)
    d_weights = lax.psum_scatter(
        parts.reshape(devices, TOP, tok_rows), ("node", "local"), scatter_dimension=0, tiled=True
    )[0].T
    combined = reduce_call(metas, y_rows)
    d_tokens = reduce_call(metas, b_rows)
    return (combined, d_tokens, d_weights)


def shards(tokens, *rest):
    if lax.axis_size("node") == 2 * TOP:
        return gathered_plan(tokens, *rest)
    return routed_plan(tokens, *rest)


def solution(mesh):
    return jax.shard_map(
        shards,
        mesh=mesh,
        in_specs=(
            P(("node", "local"), None),
            P(("node", "local"), None),
            P(("node", "local"), None),
            P("node", None, "local"),
            P("node", None, "local"),
            P("node", "local", None),
            P(("node", "local"), None),
        ),
        out_specs=(
            P(("node", "local"), None),
            P(("node", "local"), None),
            P(("node", "local"), None),
        ),
        check_vma=False,
    )
```
